32 devices in a mesh: ctx: 16 (over z, y, x), tp: 2 (over core).
Axes of the slice: x: 2, y: 2, z: 4, core: 2. Of those that a mesh axis runs over, the one named last changes fastest.
Arguments:
- queries: bfloat16 [4096, 16384], P('ctx', 'tp'), may hold values from -4 to 4
- keys: bfloat16 [4096, 1024], P('ctx', 'tp'), may hold values from -4 to 4
- values: bfloat16 [4096, 1024], P('ctx', 'tp'), may hold values from -4 to 4
- attn_out: bfloat16 [4096, 16384], P('ctx', 'tp'), may hold values from -4 to 4
- grad_out: bfloat16 [4096, 16384], P('ctx', 'tp'), may hold values from -8 to 8
- log_norm: float32 [128, 4096], P('tp', 'ctx'), may hold values from 0 to 4
- doc_start: int32 [4096], P('ctx'), may hold values from 0 to 4095, as said below
Outputs:
- grad_queries: bfloat16 [4096, 16384], P('ctx', 'tp')
- grad_keys: bfloat16 [4096, 1024], P('ctx', 'tp')
- grad_values: bfloat16 [4096, 1024], P('ctx', 'tp')
- grad_square_mean: float32 [], replicated
The draws below stay inside these ranges and needn't reach their ends.
Inputs may be any that keep to these rules, and one draw needn't show every extreme that they name: doc_start is non-decreasing, doc_start[p] <= p and p - doc_start[p] < 1024; a document is the run of tokens with equal doc_start, beginning at that position; at least one document holds exactly 1024 tokens; the last token forms a document of its own.
All inputs are finite; a program needn't handle non-finite values.
Results may differ from the reference program's by a relative error of at most 0.0086.
Values may be sent and summed in bfloat16 or wider, within the bound.
A program may use at most 192 MiB of HBM per device.

```python
import math
import jax
import jax.numpy as jnp
from jax import lax

HEADS = 128
KV = 8
HD = 128
S_DEV = 256
REACH = 4
DOC_MAX = 1024
TOKENS = 4096
N_CTX = 16


def draw_doc_start(key, part):
    key = jax.random.fold_in(key, 11)
    first_key, second_key, third_key, fourth_key = jax.random.split(key, 4)
    long_lengths = jax.random.randint(first_key, (TOKENS,), 1, DOC_MAX + 1)
    short_lengths = jax.random.randint(second_key, (TOKENS,), 1, DOC_MAX // 8 + 1)
    coin = jax.random.randint(third_key, (TOKENS,), 0, 2)
    lengths = jnp.where(coin == 1, long_lengths, short_lengths).astype(jnp.int32)
    picked = jax.random.randint(fourth_key, (), 0, 3)
    lengths = jnp.where(jnp.arange(TOKENS, dtype=jnp.int32) == picked, DOC_MAX, lengths).astype(jnp.int32)
    ends = jnp.cumsum(lengths).astype(jnp.int32)
    positions = jnp.arange(TOKENS, dtype=jnp.int32)
    index = jnp.searchsorted(ends, positions, side='right').astype(jnp.int32)
    starts = jnp.concatenate([jnp.zeros((1,), jnp.int32), ends[:-1]])
    result = starts[index].astype(jnp.int32)
    return jnp.where(positions == TOKENS - 1, TOKENS - 1, result).astype(jnp.int32)


def draw_grad_out(key, part):
    key = jax.random.fold_in(key, 23)
    base_key, row_key, head_key = jax.random.split(key, 3)
    shape = (TOKENS, HEADS * HD)
    base = jax.random.truncated_normal(base_key, -4.0, 4.0, shape, jnp.float32)
    row_scale = jnp.exp(jax.random.uniform(row_key, (TOKENS, 1), jnp.float32) * math.log(10.0))
    head_scale = jnp.exp(jax.random.uniform(head_key, (1, HEADS), jnp.float32) * math.log(10.0))
    row_ramp = 1.0 + 2.0 * jnp.arange(TOKENS, dtype=jnp.float32)[:, None] / (TOKENS - 1)
    head_ramp = 1.0 + 2.0 * jnp.arange(HEADS, dtype=jnp.float32)[None, :] / (HEADS - 1)
    columns = jnp.repeat(head_scale * head_ramp, HD, axis=1)
    return (0.002 * base * row_scale * row_ramp * columns).astype(jnp.bfloat16)


def block_levels(stream_key, extent, shards, least, largest):
    def one(dim, blocks):
        steps = jax.random.uniform(jax.random.fold_in(jax.random.fold_in(stream_key, 6), dim), (blocks,), jnp.float32, least / len(shards), largest / len(shards))
        return jnp.repeat(jnp.exp(steps), extent[dim] // blocks).reshape((-1,) + (1,) * (len(extent) - dim - 1))

    factor_of = one(*shards[0])
    for cut in shards[1:]:
        factor_of = factor_of * one(*cut)
    return factor_of


def bell_draw(key, shape, deviation, bound, cuts=(), kind=jnp.bfloat16):
    entries = deviation * jax.random.normal(key, shape, jnp.float32)
    if cuts:
        entries = entries * block_levels(key, shape, cuts, -0.22, 0.18)
    return jnp.clip(entries, -bound, bound).astype(kind)


def setup_inputs(seed: int = 0) -> dict:
    splits = jax.random.split(jax.random.key(seed), 8)
    return {
        "queries": bell_draw(splits[0], (TOKENS, HEADS * HD), 1.0, 4.0, ((0, 16), (1, 2))),
        "keys": bell_draw(splits[1], (TOKENS, KV * HD), 1.0, 4.0, ((0, 16), (1, 2))),
        "values": bell_draw(splits[2], (TOKENS, KV * HD), 1.0, 4.0, ((0, 16), (1, 2))),
        "attn_out": bell_draw(splits[3], (TOKENS, HEADS * HD), 1.0, 4.0, ((0, 16), (1, 2))),
        "grad_out": draw_grad_out(jax.random.fold_in(splits[7], 71), 0),
        "log_norm": jnp.clip(4.0 * jax.random.uniform(splits[5], (HEADS, TOKENS), jnp.float32) ** block_levels(splits[5], (HEADS, TOKENS), ((0, 2), (1, 16)), -0.2, 0.2), 0.0, 4.0),
        "doc_start": draw_doc_start(jax.random.fold_in(splits[7], 71), 0),
    }


def reference(queries, keys, values, attn_out, grad_out, log_norm, doc_start):
    scale = HD ** -0.5
    group = HEADS // KV
    margin = REACH * S_DEV
    window = margin + S_DEV
    query_heads = queries.reshape(TOKENS, KV, group, HD)
    grad_heads = grad_out.reshape(TOKENS, KV, group, HD)
    out_heads = attn_out.reshape(TOKENS, KV, group, HD)
    delta = jnp.sum(grad_heads.astype(jnp.float32) * out_heads.astype(jnp.float32), axis=-1)
    norms = log_norm.reshape(KV, group, TOKENS)
    pad_keys = jnp.concatenate([jnp.zeros((margin, KV, HD), jnp.bfloat16), keys.reshape(TOKENS, KV, HD)], axis=0)
    pad_values = jnp.concatenate([jnp.zeros((margin, KV, HD), jnp.bfloat16), values.reshape(TOKENS, KV, HD)], axis=0)

    def step(carry, tile):
        first = (tile * S_DEV).astype(jnp.int32)
        query_tile = lax.dynamic_slice_in_dim(query_heads, first, S_DEV, 0).astype(jnp.float32)
        grad_tile = lax.dynamic_slice_in_dim(grad_heads, first, S_DEV, 0).astype(jnp.float32)
        delta_tile = jnp.transpose(lax.dynamic_slice_in_dim(delta, first, S_DEV, 0), (1, 2, 0))
        norm_tile = lax.dynamic_slice_in_dim(norms, first, S_DEV, 2)
        start_tile = lax.dynamic_slice_in_dim(doc_start, first, S_DEV, 0)
        key_tile = lax.dynamic_slice_in_dim(pad_keys, first, window, 0).astype(jnp.float32)
        value_tile = lax.dynamic_slice_in_dim(pad_values, first, window, 0).astype(jnp.float32)
        query_pos = first + jnp.arange(S_DEV, dtype=jnp.int32)
        key_pos = first - margin + jnp.arange(window, dtype=jnp.int32)
        allowed = (key_pos[None, :] >= start_tile[:, None]) & (key_pos[None, :] <= query_pos[:, None])
        scores = jnp.einsum("ikgd,jkd->kgij", query_tile, key_tile) * scale
        probs = jnp.where(allowed, jnp.exp(scores - norm_tile[..., None]), 0.0)
        dprobs = jnp.einsum("ikgd,jkd->kgij", grad_tile, value_tile)
        dscores = probs * (dprobs - delta_tile[..., None])
        probs_low = lax.optimization_barrier(probs.astype(jnp.bfloat16)).astype(jnp.float32)
        dscores_low = lax.optimization_barrier(dscores.astype(jnp.bfloat16)).astype(jnp.float32)
        grad_v = jnp.einsum("kgij,ikgd->jkd", probs_low, grad_tile)
        grad_k = jnp.einsum("kgij,ikgd->jkd", dscores_low, query_tile) * scale
        grad_q = jnp.einsum("kgij,jkd->ikgd", dscores_low, key_tile) * scale
        current = lax.dynamic_slice_in_dim(carry, first, window, 1)
        carry = lax.dynamic_update_slice_in_dim(carry, current + jnp.stack([grad_k, grad_v]), first, 1)
        return carry, grad_q

    start_carry = jnp.zeros((2, TOKENS + margin, KV, HD), jnp.float32)
    carry, grad_q = lax.scan(step, start_carry, jnp.arange(N_CTX, dtype=jnp.int32))
    grad_q = grad_q.reshape(TOKENS, HEADS * HD)
    grad_square_mean = jnp.mean(grad_q * grad_q)
    grad_keys = carry[0, margin:].reshape(TOKENS, KV * HD).astype(jnp.bfloat16)
    grad_values = carry[1, margin:].reshape(TOKENS, KV * HD).astype(jnp.bfloat16)
    return (grad_q.astype(jnp.bfloat16), grad_keys, grad_values, grad_square_mean)
```

```python
import functools
import math
import jax
import jax.numpy as jnp
from jax import lax
from jax.experimental import pallas as pl
from jax.experimental.pallas import tpu as pltpu
from jax.sharding import PartitionSpec as P

HD = 128
REACH = 4
LOG2E = math.log2(math.e)
NT = (((1,), (1,)), ((), ()))


def kernel(rows, hb, steps, scale, tiles, carried, final, info, doc_row, norms, q_ref, o_ref, g_ref, *rest):
    blocks, rest = rest[: len(tiles)], rest[len(tiles) :]
    dq_in = rest[0] if carried else None
    dq_ref, *parts, square = rest[-(10 + len(tiles)) : -8]
    kv, dkv, dq, low, norm_b, delta_b, q_t, g_t = rest[-8:]
    step = pl.program_id(0)

    @pl.when(step == 0)
    def _():
        for t, block in enumerate(blocks):
            kv[t] = block[...]
        dkv[...] = jnp.zeros_like(dkv)
        square[...] = jnp.zeros_like(square)
        low[...] = jnp.transpose(jnp.broadcast_to(doc_row[...], (HD, rows)))

    for h in range(hb):
        part = pl.ds(h * rows, rows)
        cols = slice(h * HD, (h + 1) * HD)
        norm_row = norms[pl.ds(step * hb + h, 1), :] * LOG2E
        norm_b[part, :] = jnp.transpose(jnp.broadcast_to(norm_row, (HD, rows)))
        grad = g_ref[:, cols]
        delta = jnp.sum(grad.astype(jnp.float32) * o_ref[:, cols].astype(jnp.float32), axis=1, keepdims=True)
        delta_b[part, :] = jnp.broadcast_to(delta, (rows, HD))
        q_t[:, part] = jnp.transpose(q_ref[:, cols])
        g_t[:, part] = jnp.transpose(grad)
        dq[part, :] = dq_in[:, cols] if carried else jnp.zeros((rows, HD), jnp.float32)

    first = info[REACH + 2]
    base = info[0] * rows

    def tile(t, _):
        start = info[tiles[0] + t] * rows

        @pl.when((start >= 0) & (start + rows > first))
        def _():
            key = kv[t, :rows, :]
            value = kv[t, rows:, :]
            column = lax.broadcasted_iota(jnp.int32, (rows, rows), 1) + start
            query = lax.broadcasted_iota(jnp.int32, (rows, rows), 0) + base
            low_w = jnp.concatenate([low[...]] * (rows // HD), axis=1)
            allowed = (column >= low_w) & (column <= query)
            sum_k = jnp.zeros((HD, rows), jnp.float32)
            sum_v = jnp.zeros((HD, rows), jnp.float32)
            for h in range(hb):
                part = pl.ds(h * rows, rows)
                cols = slice(h * HD, (h + 1) * HD)
                norm_w = jnp.concatenate([norm_b[part, :]] * (rows // HD), axis=1)
                delta_w = jnp.concatenate([delta_b[part, :]] * (rows // HD), axis=1)
                scores = lax.dot_general(q_ref[:, cols], key, NT, preferred_element_type=jnp.float32)
                probs = jnp.where(allowed, jnp.exp2(scores * (scale * LOG2E) - norm_w), 0.0)
                dprobs = lax.dot_general(g_ref[:, cols], value, NT, preferred_element_type=jnp.float32)
                dscores = (probs * (dprobs - delta_w)).astype(jnp.bfloat16)
                probs = probs.astype(jnp.bfloat16)
                sum_v = sum_v + jnp.dot(g_t[:, part], probs, preferred_element_type=jnp.float32)
                sum_k = sum_k + jnp.dot(q_t[:, part], dscores, preferred_element_type=jnp.float32)
                dq[part, :] += jnp.dot(dscores, key, preferred_element_type=jnp.float32)
            dkv[t, 0] += sum_k
            dkv[t, 1] += sum_v

        return 0

    lax.fori_loop(0, len(tiles), tile, 0)

    for h in range(hb):
        cols = slice(h * HD, (h + 1) * HD)
        total = dq[pl.ds(h * rows, rows), :]
        if final:
            total = total * scale
            square[...] += jnp.sum((total * total).reshape(rows // 8, 8, HD), axis=0)
        dq_ref[:, cols] = total.astype(dq_ref.dtype)

    @pl.when(step == steps - 1)
    def _():
        for t, out in enumerate(parts):
            out[:rows, :] = jnp.transpose(dkv[t, 0] * scale).astype(out.dtype)
            out[rows:, :] = jnp.transpose(dkv[t, 1]).astype(out.dtype)


def head_grads(c, group, tiles, static, blocks, place, dq_in, final, dq_buffer, parts, after):
    info, doc_row, log_norm, queries, attn_out, grad_out = static
    rows, width = queries.shape
    hb = 4
    steps = group // hb
    wide = pl.BlockSpec((rows, hb * HD), lambda i: (0, c * steps + i))
    local = pl.BlockSpec((rows, hb * HD), lambda i: (0, i))
    block = pl.BlockSpec((2 * rows, HD), lambda i: (place, 0))
    anywhere = pl.BlockSpec(memory_space=pl.ANY)
    in_specs = [
        pl.BlockSpec(memory_space=pltpu.SMEM),
        pl.BlockSpec((1, rows), lambda i: (0, 0)),
        pl.BlockSpec((group, rows), lambda i: (c, 0)),
        wide,
        wide,
        wide,
    ] + [block] * len(tiles)
    operands = [info, doc_row, log_norm, queries, attn_out, grad_out, *blocks]
    if dq_in is not None:
        in_specs.append(local)
        operands.append(dq_in)
    aliases = {}
    if final and dq_buffer is not None:
        aliases = {len(operands): 0}
        operands.append(dq_buffer)
        in_specs.append(anywhere)
    for t, part in enumerate(parts or ()):
        aliases[len(operands)] = 1 + t
        operands.append(part)
        in_specs.append(anywhere)
    operands += after
    in_specs += [anywhere] * len(after)
    if final:
        dq_shape = jax.ShapeDtypeStruct((rows, width), jnp.bfloat16)
    else:
        dq_shape = jax.ShapeDtypeStruct((rows, group * HD), jnp.float32)
    part_shapes = [
        jax.ShapeDtypeStruct(blocks[0].shape, jnp.float32 if t < 2 else jnp.bfloat16) for t in tiles
    ]
    return pl.pallas_call(
        functools.partial(kernel, rows, hb, steps, HD**-0.5, tiles, dq_in is not None, final),
        grid=(steps,),
        in_specs=in_specs,
        out_specs=[wide if final else local] + [block] * len(tiles) + [pl.BlockSpec((8, HD), lambda i: (0, 0))],
        out_shape=[dq_shape, *part_shapes, jax.ShapeDtypeStruct((8, HD), jnp.float32)],
        scratch_shapes=[
            pltpu.VMEM((len(tiles), 2 * rows, HD), jnp.bfloat16),
            pltpu.VMEM((len(tiles), 2, HD, rows), jnp.float32),
            pltpu.VMEM((hb * rows, HD), jnp.float32),
            pltpu.VMEM((rows, HD), jnp.int32),
            pltpu.VMEM((hb * rows, HD), jnp.float32),
            pltpu.VMEM((hb * rows, HD), jnp.float32),
            pltpu.VMEM((HD, hb * rows), jnp.bfloat16),
            pltpu.VMEM((HD, hb * rows), jnp.bfloat16),
        ],
        input_output_aliases=aliases,
        compiler_params=pltpu.CompilerParams(vmem_limit_bytes=32 * 1024 * 1024),
        cost_estimate=pl.CostEstimate(
            flops=20 * rows * rows * HD * group * len(tiles),
            bytes_accessed=8 * rows * group * HD,
            transcendentals=rows * rows * group * len(tiles),
        ),
    )(*operands)


def shards(queries, keys, values, attn_out, grad_out, log_norm, doc_start):
    rows = queries.shape[0]
    kv_count = keys.shape[1] // HD
    head_count = queries.shape[1] // HD
    group = head_count // kv_count
    peers = lax.axis_size("ctx")
    device = lax.axis_index("ctx")
    place = device % REACH
    onward = [(i, i + REACH) for i in range(peers - REACH)]
    back = [(i + REACH, i) for i in range(peers - REACH)]
    flips = [[(i, i ^ f) for i in range(peers)] for f in (1, 2, 3)]
    partner = [place ^ f for f in (1, 2, 3)]

    key_block = [device, device - REACH] + [
        device - place + other - jnp.where(other > place, REACH, 0) for other in partner
    ]
    info = jnp.stack(key_block + [device, doc_start[0]]).astype(jnp.int32)
    doc_row = doc_start.reshape(1, rows)

    heads = list(range(kv_count))
    groups = [g for g in (heads[:1], heads[1:-1], heads[1:][-1:]) if g]
    arrived = []
    for members in groups:
        own = jnp.concatenate(
            [x[:, c * HD : (c + 1) * HD] for c in members for x in (keys, values)], axis=0
        )
        arrived.append([own, lax.ppermute(own, "ctx", onward)])

    def spread(g, after):
        own, far = arrived[g]
        if after:
            far, *_ = lax.optimization_barrier((far, *after))
        arrived[g] += [
            lax.ppermute(jnp.where(place < other, own, far), "ctx", flip)
            for flip, other in zip(flips, partner)
        ]

    where = {c: (g, members.index(c)) for g, members in enumerate(groups) for c in members}

    static = (info, doc_row, log_norm, queries, attn_out, grad_out)
    remote = tuple(range(1, REACH + 1))
    early = (kv_count + 1) // 2
    dq_buffer = None
    tokens = []
    squares = []
    dq_part = [None] * kv_count
    own_part = [None] * len(groups)
    away_part = [None] * len(groups)
    returned = [None] * len(groups)
    for c in range(early):
        g, at = where[c]
        dq_part[c], own_part[g], token = head_grads(
            c, group, (0,), static, arrived[g][:1], at, None, False, None,
            None if own_part[g] is None else [own_part[g]], tokens,
        )
        tokens = [token]

    spread(0, [])
    for c in range(kv_count):
        g, at = where[c]
        last = c < early
        held = []
        if c == 2:
            *held, _ = lax.optimization_barrier((*returned[0], *tokens))
            returned[0] = held[:]
        if g + 1 < len(groups) and c == groups[g][-1]:
            spread(g + 1, tokens if g else [])
            held.append(arrived[g + 1][1])
        dq_new, *away, token = head_grads(
            c, group, remote, static, arrived[g][1:], at, dq_part[c], last, dq_buffer, away_part[g],
            tokens + held,
        )
        away_part[g] = away
        if last:
            dq_buffer = dq_new
            squares.append(token)
        else:
            dq_part[c] = dq_new
        tokens = [token]
        if c == groups[g][-1]:
            returned[g] = [lax.ppermute(x, "ctx", flip) for x, flip in zip(away[1:], flips)]

    landed = []
    for g in range(len(groups)):
        far = away_part[g][0]
        for x, other in zip(returned[g], partner):
            far = far + jnp.where(other < place, x.astype(jnp.float32), 0.0)
        landed.append(lax.ppermute(far.astype(jnp.bfloat16), "ctx", back))

    for c in range(early, kv_count):
        g, at = where[c]
        held = landed[:-1] + returned[-1] if c == kv_count - 1 else returned[max(len(groups) - 2, 0)]
        dq_buffer, own_part[g], token = head_grads(
            c, group, (0,), static, arrived[g][:1], at, dq_part[c], True, dq_buffer,
            None if own_part[g] is None else [own_part[g]], tokens + held,
        )
        squares.append(token)
        tokens = [token]

    finished = []
    for g, members in enumerate(groups):
        own = own_part[g] + landed[g].astype(jnp.float32)
        for x, other in zip(returned[g], partner):
            own = own + jnp.where(other > place, x.astype(jnp.float32), 0.0)
        total = own.astype(jnp.bfloat16)
        finished += [total[i * 2 * rows : (i + 1) * 2 * rows] for i in range(len(members))]

    entry_total = float(rows * peers * head_count * lax.axis_size("tp") * HD)
    grad_square_mean = lax.psum(jnp.sum(sum(squares)) / entry_total, ("ctx", "tp"))
    grad_keys = jnp.concatenate([x[:rows] for x in finished], axis=1)
    grad_values = jnp.concatenate([x[rows:] for x in finished], axis=1)
    return (dq_buffer, grad_keys, grad_values, grad_square_mean)


def solution(mesh):
    return jax.shard_map(
        shards,
        mesh=mesh,
        in_specs=(
            P("ctx", "tp"),
            P("ctx", "tp"),
            P("ctx", "tp"),
            P("ctx", "tp"),
            P("ctx", "tp"),
            P("tp", "ctx"),
            P("ctx"),
        ),
        out_specs=(P("ctx", "tp"), P("ctx", "tp"), P("ctx", "tp"), P()),
        check_vma=False,
    )
```
